32 devices in a mesh: down: 8 (over y, x, core), cross: 4 (over z).
Axes of the slice: x: 2, y: 2, z: 4, core: 2. Of those that a mesh axis runs over, the one named last changes fastest.
Arguments:
- fields: float32 [4, 64, 256, 128], P(None, 'down', 'cross'), may hold values from -4 to 4
- embers: float32 [7, 8, 4, 6, 256], P(None, 'down', 'cross'), may hold values from 0.05 to 1
- counts: int32 [8, 4, 6], P('down', 'cross'), may hold values from 0 to 256, as said below
Outputs:
- advanced: float32 [4, 64, 256, 128], P(None, 'down', 'cross')
- landed: float32 [4, 8, 4, 6, 256], P(None, 'down', 'cross')
The draws below stay inside these ranges and needn't reach their ends.
Inputs may be any that keep to these rules, and one draw needn't show every extreme that they name: `counts`: live records fill the leading slots of a buffer; some buffer is full in every draw.
All inputs are finite; a program needn't handle non-finite values.
Results may differ from the reference program's by a relative error of at most 0.0003.
Values sent between devices are 32-bit elements; how exact they have to be, the bound alone decides.
A program may use at most 64 MiB of HBM per device.

```python
import jax
import jax.numpy as jnp
from jax import lax

CX = 8
CY = 64
NZ = 128
STEPS = 6
SLOTS = 6
CAP = 256
TD = 8
TC = 4
NX = 64
NY = 256


def draw_counts(key, part):
    band_key, front_key, quiet_key = jax.random.split(key, 3)
    band_start = jax.random.randint(band_key, (), 0, TD)
    band_width = max(1, TD // 8)
    tile_rows = jnp.arange(TD)[:, None, None]
    in_front = (tile_rows - band_start) % TD < band_width
    front_counts = jax.random.randint(front_key, (TD, TC, SLOTS), CAP // 2, CAP + 1)
    quiet_counts = jax.random.randint(quiet_key, (TD, TC, SLOTS), 0, CAP // 4 + 1)
    counts = jnp.where(in_front, front_counts, quiet_counts)
    full_slot = (tile_rows == band_start) & (jnp.arange(TC)[None, :, None] == 0) & (jnp.arange(SLOTS)[None, None, :] == 0)
    return jnp.where(full_slot, CAP, counts).astype(jnp.int32)


def level_of(stream_key, dims, cuts, low, largest):
    loudness, own = 1.0, jax.random.fold_in(stream_key, 6)
    for dim, shards_of in cuts:
        draws = jnp.exp(jax.random.uniform(jax.random.fold_in(own, dim), (shards_of,), jnp.float32, low / len(cuts), largest / len(cuts)))
        loudness = loudness * jnp.repeat(draws, dims[dim] // shards_of).reshape([-1 if axis == dim else 1 for axis in range(len(dims))])
    return loudness


def gaussian(key, extent, width, reach, pieces=(), kind=jnp.bfloat16):
    loudness = level_of(key, extent, pieces, -0.22, 0.18) if pieces else 1.0
    result = jax.random.normal(key, extent, jnp.float32) * width * loudness
    return jnp.minimum(jnp.maximum(result, -reach), reach).astype(kind)


def setup_inputs(seed: int = 0) -> dict:
    seeds = jax.random.split(jax.random.key(seed), 4)
    return {
        "fields": gaussian(seeds[0], (4, NX, NY, NZ), 1.0, 4.0, ((1, 8), (2, 4)), jnp.float32),
        "embers": jnp.clip(0.05 + 0.95 * jax.random.uniform(seeds[1], (7, TD, TC, SLOTS, CAP), jnp.float32) ** level_of(seeds[1], (7, TD, TC, SLOTS, CAP), ((1, 8), (2, 4)), -0.2, 0.2), 0.05, 1.0),
        "counts": draw_counts(jax.random.fold_in(seeds[3], 71), 0),
    }


HORIZONTAL_MIX = 0.1
VERTICAL_MIX = 0.1
ADVECTION = 0.25
DRAG_RATE = 0.6
BURN_RATE = 0.5
HEAT_YIELD = 4.0
DESTINATIONS = ((1, -1), (1, 0), (1, 1), (2, -1), (2, 0), (2, 1))


def advance(padded):
    centre = padded[:, 1:-1, 1:-1]
    eastern = padded[:, 2:, 1:-1]
    western = padded[:, :-2, 1:-1]
    northern = padded[:, 1:-1, 2:]
    southern = padded[:, 1:-1, :-2]
    upper_level = jnp.concatenate([centre[..., 1:], centre[..., -1:]], axis=-1)
    lower_level = jnp.concatenate([centre[..., :1], centre[..., :-1]], axis=-1)
    spread = eastern + western + northern + southern - 4.0 * centre
    column_mix = upper_level + lower_level - 2.0 * centre
    carried = centre[0:1] * (eastern - western) * 0.5 + centre[1:2] * (northern - southern) * 0.5
    return centre + HORIZONTAL_MIX * spread + VERTICAL_MIX * column_mix - ADVECTION * carried


def tent_weights(position, cell_count):
    centres = jnp.arange(cell_count).astype(jnp.float32) + 0.5
    return jnp.maximum(0.0, 1.0 - jnp.abs(position[:, None] - centres[None, :]))


def ember_update(tile_fields, records):
    cells_down = tile_fields.shape[1]
    cells_cross = tile_fields.shape[2]
    levels = tile_fields.shape[3]
    weight_down = tent_weights(records[0] * cells_down, cells_down)
    weight_cross = tent_weights(records[1] * cells_cross, cells_cross)
    weight_level = tent_weights(records[2] * levels, levels)
    column = jnp.einsum("kxyz,ez->kxye", tile_fields, weight_level, precision=lax.Precision.HIGHEST)
    across = jnp.sum(column * weight_cross.T[None, None], axis=2)
    sampled = jnp.sum(across * weight_down.T[None], axis=1)
    ember_mass = records[5]
    burned = ember_mass * BURN_RATE * jax.nn.sigmoid(records[6] + sampled[2] - sampled[3])
    living = (ember_mass > 0.0).astype(tile_fields.dtype)
    landed = jnp.stack([
        records[3] + DRAG_RATE * (sampled[0] - records[3]),
        records[4] + DRAG_RATE * (sampled[1] - records[4]),
        records[6] + DRAG_RATE * (sampled[2] - records[6]),
        ember_mass - burned,
    ]) * living[None]
    spread = weight_down[:, :, None] * weight_cross[:, None, :] * (HEAT_YIELD * burned)[:, None, None]
    spread = spread.reshape(records.shape[1], cells_down * cells_cross)
    deposit = jnp.dot(spread.T, weight_level, precision=lax.Precision.HIGHEST)
    return landed, deposit.reshape(cells_down, cells_cross, levels)


def one_tile(tile_pair):
    return ember_update(tile_pair[0], tile_pair[1])


def reference(fields, embers, counts):
    slot_index = jnp.arange(CAP).astype(jnp.int32)
    live_mask = (slot_index[None, None, None, :] < counts[..., None]).astype(jnp.float32)
    outgoing = embers * live_mask[None]
    arrivals = []
    for target in range(SLOTS):
        down_step, cross_step = DESTINATIONS[target]
        shifted = outgoing[:, :, :, target]
        shifted = jnp.pad(shifted, ((0, 0), (down_step, 0), (0, 0), (0, 0)))[:, :TD]
        if cross_step > 0:
            shifted = jnp.pad(shifted, ((0, 0), (0, 0), (cross_step, 0), (0, 0)))[:, :, :TC]
        elif cross_step < 0:
            shifted = jnp.pad(shifted, ((0, 0), (0, 0), (0, -cross_step), (0, 0)))[:, :, -cross_step:]
        arrivals.append(shifted)
    arrived = jnp.stack(arrivals, axis=3)
    tile_fields = fields.reshape(4, TD, CX, TC, CY, NZ).transpose(1, 3, 0, 2, 4, 5).reshape(TD * TC, 4, CX, CY, NZ)
    tile_records = arrived.transpose(1, 2, 0, 3, 4).reshape(TD * TC, 7, SLOTS * CAP)
    landed, deposit = lax.map(one_tile, (tile_fields, tile_records))
    landed = landed.reshape(TD, TC, 4, SLOTS, CAP).transpose(2, 0, 1, 3, 4)
    deposit = deposit.reshape(TD, TC, CX, CY, NZ).transpose(0, 2, 1, 3, 4).reshape(NX, NY, NZ)
    current = fields
    for step_index in range(STEPS):
        padded = jnp.pad(current, ((0, 0), (1, 1), (1, 1), (0, 0)))
        current = advance(padded)
    advanced = jnp.concatenate([current[:2], current[2:3] + deposit[None], current[3:]], axis=0)
    return advanced, landed
```

```python
import functools

import jax
import jax.numpy as jnp
from jax import lax
from jax.experimental import pallas as pl
from jax.experimental.pallas import tpu as pltpu
from jax.sharding import PartitionSpec as P

STEPS = 6
HORIZONTAL_MIX = 0.1
VERTICAL_MIX = 0.1
ADVECTION = 0.25
DRAG_RATE = 0.6
BURN_RATE = 0.5
HEAT_YIELD = 4.0
DESTINATIONS = ((1, -1), (1, 0), (1, 1), (2, -1), (2, 0), (2, 1))
PAD = 8
CHUNK = 32
MESH = pl.DeviceIdType.MESH


def halves(x):
    high = x.astype(jnp.bfloat16)
    return high, (x - high.astype(jnp.float32)).astype(jnp.bfloat16)


def tent(position, cells):
    centres = lax.broadcasted_iota(jnp.int32, (cells, position.shape[1]), 0).astype(jnp.float32) + 0.5
    return jnp.maximum(0.0, 1.0 - jnp.abs(position - centres))


def kernel(
    nd, nc, fields_ref, embers_ref, counts_ref, advanced_ref, landed_ref,
    state, ysend, yrecv, esend, erecv, split, spread, deposit,
    in_sem, x_send, x_recv, y_send, y_recv, e_send, e_recv,
):
    fields, cx, cy, nz = fields_ref.shape
    slots, capacity = embers_ref.shape[3:]
    d = lax.axis_index("down")
    c = lax.axis_index("cross")
    rows = pl.ds(PAD, cy)

    def inside(a, b):
        return (d + a >= 0) & (d + a < nd) & (c + b >= 0) & (c + b < nc)

    loading = pltpu.make_async_copy(fields_ref, state.at[0, :, pl.ds(1, cx), rows], in_sem)
    loading.start()

    zero_row = jnp.zeros((cy, nz), jnp.float32)
    for b in range(2):
        for k in range(fields):
            state[b, k, 0, PAD:PAD + cy, :] = zero_row
            state[b, k, cx + 1, PAD:PAD + cy, :] = zero_row
    yrecv[...] = jnp.zeros(yrecv.shape, jnp.float32)
    erecv[...] = jnp.zeros(erecv.shape, jnp.float32)

    barrier = pltpu.get_barrier_semaphore()
    peers = [(a, b) for a in (-2, -1, 1, 2) for b in (-1, 0, 1)] + [(0, -1), (0, 1)]
    present = 0
    for a, b in peers:
        there = inside(a, b)
        present = present + there.astype(jnp.int32)

        @pl.when(there)
        def _(a=a, b=b):
            pl.semaphore_signal(barrier, inc=1, device_id=(d + a, c + b), device_id_type=MESH)

    lane = lax.broadcasted_iota(jnp.int32, (1, capacity), 1)
    for j in range(slots):
        live = lane < counts_ref[0, 0, j]
        for i in range(7):
            esend[j, i:i + 1, :] = jnp.where(live, embers_ref[i, 0, 0, j:j + 1, :], 0.0)
        esend[j, 7:8, :] = jnp.zeros((1, capacity), jnp.float32)

    def x_copy(b, side):
        source, target, by = ((cx, 0, 1), (1, cx + 1, -1))[side]
        return pltpu.make_async_remote_copy(
            src_ref=state.at[b, :, source, rows],
            dst_ref=state.at[b, :, target, rows],
            send_sem=x_send.at[b, side], recv_sem=x_recv.at[b, side],
            device_id=(d + by, c), device_id_type=MESH,
        )

    def y_copy(b, side):
        by = (1, -1)[side]
        return pltpu.make_async_remote_copy(
            src_ref=ysend.at[b, side], dst_ref=yrecv.at[b, side],
            send_sem=y_send.at[b, side], recv_sem=y_recv.at[b, side],
            device_id=(d, c + by), device_id_type=MESH,
        )

    def e_copy(j):
        a, b = DESTINATIONS[j]
        return pltpu.make_async_remote_copy(
            src_ref=esend.at[j], dst_ref=erecv.at[j],
            send_sem=e_send.at[j], recv_sem=e_recv.at[j],
            device_id=(d + a, c + b), device_id_type=MESH,
        )

    def start_x(b):
        for side, by in enumerate((1, -1)):
            @pl.when(inside(by, 0))
            def _(side=side):
                x_copy(b, side).start()

    def wait_x(b):
        for side, by in enumerate((1, -1)):
            @pl.when(inside(-by, 0))
            def _(side=side):
                x_copy(b, side).wait_recv()

            @pl.when(inside(by, 0))
            def _(side=side):
                x_copy(b, side).wait_send()

    def start_y(b):
        for k in range(fields):
            for i in range(cx):
                ysend[b, 0, k, i:i + 1, :] = state[b, k, i + 1, PAD + cy - 1:PAD + cy, :]
                ysend[b, 1, k, i:i + 1, :] = state[b, k, i + 1, PAD:PAD + 1, :]
        for side, by in enumerate((1, -1)):
            @pl.when(inside(0, by))
            def _(side=side):
                y_copy(b, side).start()

    def wait_y(b):
        for side, by in enumerate((1, -1)):
            @pl.when(inside(0, -by))
            def _(side=side):
                y_copy(b, side).wait_recv()

            @pl.when(inside(0, by))
            def _(side=side):
                y_copy(b, side).wait_send()

        for k in range(fields):
            for i in range(cx):
                state[b, k, i + 1, PAD - 1:PAD, :] = yrecv[b, 0, k, i:i + 1, :]
                state[b, k, i + 1, PAD + cy:PAD + cy + 1, :] = yrecv[b, 1, k, i:i + 1, :]

    level = lax.broadcasted_iota(jnp.int32, (CHUNK, nz), 1)
    keep = 1.0 - 4.0 * HORIZONTAL_MIX - 2.0 * VERTICAL_MIX

    def stencil(b, i, last):
        for y in range(0, cy, CHUNK):
            here = slice(PAD + y, PAD + y + CHUNK)
            u = state[b, 0, i, here, :] * (0.5 * ADVECTION)
            v = state[b, 1, i, here, :] * (0.5 * ADVECTION)
            for k in range(fields):
                centre = state[b, k, i, here, :]
                eastern = state[b, k, i + 1, here, :]
                western = state[b, k, i - 1, here, :]
                northern = state[b, k, i, PAD + y + 1:PAD + y + 1 + CHUNK, :]
                southern = state[b, k, i, PAD + y - 1:PAD + y - 1 + CHUNK, :]
                upper = jnp.where(level == nz - 1, centre, pltpu.roll(centre, nz - 1, 1))
                lower = jnp.where(level == 0, centre, pltpu.roll(centre, 1, 1))
                new = (
                    keep * centre
                    + HORIZONTAL_MIX * ((eastern + western) + (northern + southern))
                    + VERTICAL_MIX * (upper + lower)
                    - (u * (eastern - western) + v * (northern - southern))
                )
                if not last:
                    state[1 - b, k, i, here, :] = new
                else:
                    if k == 2:
                        new = new + deposit[pl.ds(pl.multiple_of((i - 1) * cy + y, CHUNK), CHUNK), :]
                    advanced_ref[k, i - 1, y:y + CHUNK, :] = new

    def embers_of(j):
        a, b = DESTINATIONS[j]

        @pl.when(inside(-a, -b))
        def _():
            e_copy(j).wait_recv()

        @pl.when(inside(a, b))
        def _():
            e_copy(j).wait_send()

        def part(i):
            return erecv[j, i:i + 1, :]

        wx = tent(part(0) * cx, cx)
        wy = tent(part(1) * cy, cy)
        wz = tent(part(2) * nz, nz)
        z_high, z_low = halves(wz)
        z_both = jnp.concatenate([z_high, z_high], axis=0)
        for i in range(cx):
            at = slice(i * cy, (i + 1) * cy)
            spread[0, at, :], spread[1, at, :] = halves(wx[i:i + 1, :] * wy)
        sampled = []
        for k in range(fields):
            of = split[k * cx * cy:(k + 1) * cx * cy, :]
            column = jnp.dot(of, z_both, preferred_element_type=jnp.float32)
            column += jnp.dot(of[:, :nz], z_low, preferred_element_type=jnp.float32)
            across = jnp.sum(column.reshape(cx, cy, capacity) * wy[None], axis=1)
            sampled.append(jnp.sum(across * wx, axis=0, keepdims=True))
        ue, ve, mass, heat = part(3), part(4), part(5), part(6)
        burned = mass * BURN_RATE * jax.nn.sigmoid(heat + sampled[2] - sampled[3])
        living = mass > 0.0
        outs = (
            ue + DRAG_RATE * (sampled[0] - ue),
            ve + DRAG_RATE * (sampled[1] - ve),
            heat + DRAG_RATE * (sampled[2] - heat),
            mass - burned,
        )
        for i in range(4):
            landed_ref[i, 0, 0, j:j + 1, :] = jnp.where(living, outs[i], 0.0)
        g_high, g_low = halves(wz * (HEAT_YIELD * burned))

        def nt(p, q):
            return lax.dot_general(p, q, (((1,), (1,)), ((), ())), preferred_element_type=jnp.float32)

        s_high = spread[0]
        add = nt(s_high, g_high) + nt(s_high, g_low) + nt(spread[1], g_high)
        deposit[...] = add if j == 0 else deposit[...] + add

    pl.semaphore_wait(barrier, present)
    for j in range(slots):
        @pl.when(inside(*DESTINATIONS[j]))
        def _(j=j):
            e_copy(j).start()
    loading.wait()

    for step in range(STEPS):
        b = step % 2
        start_x(b)
        start_y(b)
        if step == 0:
            for k in range(fields):
                for i in range(cx):
                    at = slice((k * cx + i) * cy, (k * cx + i + 1) * cy)
                    split[at, :nz], split[at, nz:] = halves(state[0, k, i + 1, PAD:PAD + cy, :])
        embers_of(step)
        wait_y(b)
        last = step == STEPS - 1

        def inner(i, carry, b=b, last=last):
            stencil(b, i, last)
            return carry

        lax.fori_loop(2, cx, inner, 0)
        wait_x(b)
        stencil(b, 1, last)
        stencil(b, cx, last)


def solution(mesh):
    nd, nc = mesh.shape["down"], mesh.shape["cross"]

    def local(fields, embers, counts):
        k, cx, cy, nz = fields.shape
        slots, capacity = embers.shape[3:]
        sem = pltpu.SemaphoreType.DMA
        return pl.pallas_call(
            functools.partial(kernel, nd, nc),
            out_shape=(
                jax.ShapeDtypeStruct(fields.shape, jnp.float32),
                jax.ShapeDtypeStruct((4, 1, 1, slots, capacity), jnp.float32),
            ),
            in_specs=[
                pl.BlockSpec(memory_space=pl.ANY),
                pl.BlockSpec(memory_space=pltpu.VMEM),
                pl.BlockSpec(memory_space=pltpu.SMEM),
            ],
            out_specs=[pl.BlockSpec(memory_space=pltpu.VMEM)] * 2,
            scratch_shapes=[
                pltpu.VMEM((2, k, cx + 2, cy + 2 * PAD, nz), jnp.float32),
                pltpu.VMEM((2, 2, k, cx, nz), jnp.float32),
                pltpu.VMEM((2, 2, k, cx, nz), jnp.float32),
                pltpu.VMEM((slots, 8, capacity), jnp.float32),
                pltpu.VMEM((slots, 8, capacity), jnp.float32),
                pltpu.VMEM((k * cx * cy, 2 * nz), jnp.bfloat16),
                pltpu.VMEM((2, cx * cy, capacity), jnp.bfloat16),
                pltpu.VMEM((cx * cy, nz), jnp.float32),
                sem, sem((2, 2)), sem((2, 2)), sem((2, 2)), sem((2, 2)),
                sem((slots,)), sem((slots,)),
            ],
            compiler_params=pltpu.CompilerParams(
                collective_id=0, has_side_effects=True, vmem_limit_bytes=40 * 1024 * 1024
            ),
            name="fire_step",
        )(fields, embers, counts)

    placed = (
        P(None, "down", "cross", None),
        P(None, "down", "cross", None, None),
        P("down", "cross", None),
    )
    return jax.shard_map(
        local,
        mesh=mesh,
        in_specs=placed,
        out_specs=(P(None, "down", "cross", None), P(None, "down", "cross", None, None)),
        check_vma=False,
    )
```

```python
import functools

import jax
import jax.numpy as jnp
from jax import lax
from jax.experimental import pallas as pl
from jax.experimental.pallas import tpu as pltpu
from jax.sharding import PartitionSpec as P

STEPS = 6
HORIZONTAL_MIX = 0.1
VERTICAL_MIX = 0.1
ADVECTION = 0.25
DRAG_RATE = 0.6
BURN_RATE = 0.5
HEAT_YIELD = 4.0
DESTINATIONS = ((1, -1), (1, 0), (1, 1), (2, -1), (2, 0), (2, 1))
PAD = 8
CHUNK = 32
MESH = pl.DeviceIdType.MESH


def halves(x):
    high = x.astype(jnp.bfloat16)
    return high, (x - high.astype(jnp.float32)).astype(jnp.bfloat16)


def tent(position, cells):
    centres = lax.broadcasted_iota(jnp.int32, (cells, position.shape[1]), 0).astype(jnp.float32) + 0.5
    return jnp.maximum(0.0, 1.0 - jnp.abs(position - centres))


def kernel(
    nd, nc, fields_ref, embers_ref, counts_ref, advanced_ref, landed_ref,
    state, ysend, yrecv, esend, erecv, split, spread, deposit,
    in_sem, x_send, x_recv, y_send, y_recv, e_send, e_recv,
):
    fields, cx, cy, nz = fields_ref.shape
    slots, capacity = len(DESTINATIONS), embers_ref.shape[2]
    d = lax.axis_index("down")
    c = lax.axis_index("cross")
    rows = pl.ds(PAD, cy)
    parts = cy // CHUNK

    def inside(a, b):
        return (d + a >= 0) & (d + a < nd) & (c + b >= 0) & (c + b < nc)

    loading = pltpu.make_async_copy(fields_ref, state.at[0, :, pl.ds(1, cx), rows], in_sem)
    loading.start()

    zero_row = jnp.zeros((cy, nz), jnp.float32)
    for b in range(2):
        for k in range(fields):
            state[b, k, 0, PAD:PAD + cy, :] = zero_row
            state[b, k, cx + 1, PAD:PAD + cy, :] = zero_row
    yrecv[...] = jnp.zeros(yrecv.shape, jnp.float32)
    erecv[...] = jnp.zeros(erecv.shape, jnp.float32)

    barrier = pltpu.get_barrier_semaphore()
    peers = [(a, b) for a in (-2, -1, 1, 2) for b in (-1, 0, 1)] + [(0, -1), (0, 1)]
    present = 0
    for a, b in peers:
        there = inside(a, b)
        present = present + there.astype(jnp.int32)

        @pl.when(there)
        def _(a=a, b=b):
            pl.semaphore_signal(barrier, inc=1, device_id=(d + a, c + b), device_id_type=MESH)

    lane = lax.broadcasted_iota(jnp.int32, (1, capacity), 1)
    for j in range(slots):
        live = lane < counts_ref[0, 0, j]
        for i in range(7):
            esend[j, i:i + 1, :] = jnp.where(live, embers_ref[i * slots + j], 0.0)
        esend[j, 7:8, :] = jnp.zeros((1, capacity), jnp.float32)

    def x_copy(b, side, part):
        source, target, by = ((cx, 0, 1), (1, cx + 1, -1))[side]
        band = pl.ds(PAD + part * CHUNK, CHUNK)
        return pltpu.make_async_remote_copy(
            src_ref=state.at[b, :, source, band],
            dst_ref=state.at[b, :, target, band],
            send_sem=x_send.at[b, side, part], recv_sem=x_recv.at[b, side, part],
            device_id=(d + by, c), device_id_type=MESH,
        )

    def y_copy(b, side):
        by = (1, -1)[side]
        return pltpu.make_async_remote_copy(
            src_ref=ysend.at[b, side], dst_ref=yrecv.at[b, side],
            send_sem=y_send.at[b, side], recv_sem=y_recv.at[b, side],
            device_id=(d, c + by), device_id_type=MESH,
        )

    def e_copy(j):
        a, b = DESTINATIONS[j]
        return pltpu.make_async_remote_copy(
            src_ref=esend.at[j], dst_ref=erecv.at[j],
            send_sem=e_send.at[j], recv_sem=e_recv.at[j],
            device_id=(d + a, c + b), device_id_type=MESH,
        )

    def each_side(down, from_there, act):
        for side, by in enumerate((1, -1)):
            by = -by if from_there else by

            @pl.when(inside(by, 0) if down else inside(0, by))
            def _(side=side):
                act(side)

    def start_x(b, part):
        each_side(True, False, lambda side: x_copy(b, side, part).start())

    def arrive_x(b, part):
        each_side(True, True, lambda side: x_copy(b, side, part).wait_recv())

    def sent_x(b, part):
        each_side(True, False, lambda side: x_copy(b, side, part).wait_send())

    def sent_y(b):
        each_side(False, False, lambda side: y_copy(b, side).wait_send())

    def start_y(b):
        for k in range(fields):
            for i in range(cx):
                ysend[b, 0, k, i:i + 1, :] = state[b, k, i + 1, PAD + cy - 1:PAD + cy, :]
                ysend[b, 1, k, i:i + 1, :] = state[b, k, i + 1, PAD:PAD + 1, :]
        each_side(False, False, lambda side: y_copy(b, side).start())

    def arrive_y(b):
        each_side(False, True, lambda side: y_copy(b, side).wait_recv())
        for k in range(fields):
            for i in range(cx):
                state[b, k, i + 1, PAD - 1:PAD, :] = yrecv[b, 0, k, i:i + 1, :]
                state[b, k, i + 1, PAD + cy:PAD + cy + 1, :] = yrecv[b, 1, k, i:i + 1, :]

    level = lax.broadcasted_iota(jnp.int32, (CHUNK, nz), 1)
    keep = 1.0 - 4.0 * HORIZONTAL_MIX - 2.0 * VERTICAL_MIX

    def stencil(b, i, part, last):
        for y in (part * CHUNK,):
            here = slice(PAD + y, PAD + y + CHUNK)
            u = state[b, 0, i, here, :] * (0.5 * ADVECTION)
            v = state[b, 1, i, here, :] * (0.5 * ADVECTION)
            for k in range(fields):
                centre = state[b, k, i, here, :]
                eastern = state[b, k, i + 1, here, :]
                western = state[b, k, i - 1, here, :]
                northern = state[b, k, i, PAD + y + 1:PAD + y + 1 + CHUNK, :]
                southern = state[b, k, i, PAD + y - 1:PAD + y - 1 + CHUNK, :]
                upper = jnp.where(level == nz - 1, centre, pltpu.roll(centre, nz - 1, 1))
                lower = jnp.where(level == 0, centre, pltpu.roll(centre, 1, 1))
                new = (
                    keep * centre
                    + HORIZONTAL_MIX * ((eastern + western) + (northern + southern))
                    + VERTICAL_MIX * (upper + lower)
                    - (u * (eastern - western) + v * (northern - southern))
                )
                if not last:
                    state[1 - b, k, i, here, :] = new
                else:
                    if k == 2:
                        new = new + deposit[pl.ds(pl.multiple_of((i - 1) * cy + y, CHUNK), CHUNK), :]
                    advanced_ref[k, i - 1, y:y + CHUNK, :] = new

    def embers_of(j):
        a, b = DESTINATIONS[j]

        @pl.when(inside(-a, -b))
        def _():
            e_copy(j).wait_recv()

        def part(i):
            return erecv[j, i:i + 1, :]

        wx = tent(part(0) * cx, cx)
        wy = tent(part(1) * cy, cy)
        wz = tent(part(2) * nz, nz)
        z_high, z_low = halves(wz)
        z_both = jnp.concatenate([z_high, z_high], axis=0)
        for i in range(cx):
            at = slice(i * cy, (i + 1) * cy)
            spread[0, at, :], spread[1, at, :] = halves(wx[i:i + 1, :] * wy)
        sampled = []
        for k in range(fields):
            of = split[k * cx * cy:(k + 1) * cx * cy, :]
            column = jnp.dot(of, z_both, preferred_element_type=jnp.float32)
            column += jnp.dot(of[:, :nz], z_low, preferred_element_type=jnp.float32)
            across = jnp.sum(column.reshape(cx, cy, capacity) * wy[None], axis=1)
            sampled.append(jnp.sum(across * wx, axis=0, keepdims=True))
        ue, ve, mass, heat = part(3), part(4), part(5), part(6)
        burned = mass * BURN_RATE * jax.nn.sigmoid(heat + sampled[2] - sampled[3])
        living = mass > 0.0
        outs = (
            ue + DRAG_RATE * (sampled[0] - ue),
            ve + DRAG_RATE * (sampled[1] - ve),
            heat + DRAG_RATE * (sampled[2] - heat),
            mass - burned,
        )
        for i in range(4):
            landed_ref[i * slots + j] = jnp.where(living, outs[i], 0.0)
        g_high, g_low = halves(wz * (HEAT_YIELD * burned))

        def nt(p, q):
            return lax.dot_general(p, q, (((1,), (1,)), ((), ())), preferred_element_type=jnp.float32)

        s_high = spread[0]
        add = nt(s_high, g_high) + nt(s_high, g_low) + nt(spread[1], g_high)
        deposit[...] = add if j == 0 else deposit[...] + add

    pl.semaphore_wait(barrier, present)
    for j in range(slots):
        @pl.when(inside(*DESTINATIONS[j]))
        def _(j=j):
            e_copy(j).start()
    loading.wait()

    for part in range(parts):
        start_x(0, part)
    start_y(0)
    for k in range(fields):
        for i in range(cx):
            at = slice((k * cx + i) * cy, (k * cx + i + 1) * cy)
            split[at, :nz], split[at, nz:] = halves(state[0, k, i + 1, PAD:PAD + cy, :])

    for step in range(STEPS):
        b = step % 2
        last = step == STEPS - 1
        embers_of(step)
        arrive_y(b)
        for part in range(parts):
            arrive_x(b, part)
            if step > 0:
                sent_x(1 - b, part)
            stencil(b, 1, part, last)
            stencil(b, cx, part, last)
            if not last:
                start_x(1 - b, part)
            if part == 0:
                def inner(i, carry, b=b, last=last):
                    for part in range(parts):
                        stencil(b, i, part, last)
                    return carry

                lax.fori_loop(2, cx, inner, 0)
        if step > 0:
            sent_y(1 - b)
        if not last:
            start_y(1 - b)
    for part in range(parts):
        sent_x((STEPS - 1) % 2, part)
    sent_y((STEPS - 1) % 2)
    for j in range(slots):
        @pl.when(inside(*DESTINATIONS[j]))
        def _(j=j):
            e_copy(j).wait_send()


def solution(mesh):
    nd, nc = mesh.shape["down"], mesh.shape["cross"]

    def local(fields, embers, counts):
        k, cx, cy, nz = fields.shape
        slots, capacity = embers.shape[3:]
        sem = pltpu.SemaphoreType.DMA
        advanced, landed = pl.pallas_call(
            functools.partial(kernel, nd, nc),
            out_shape=(
                jax.ShapeDtypeStruct(fields.shape, jnp.float32),
                jax.ShapeDtypeStruct((4 * slots, 1, capacity), jnp.float32),
            ),
            in_specs=[
                pl.BlockSpec(memory_space=pltpu.HBM),
                pl.BlockSpec(memory_space=pltpu.VMEM),
                pl.BlockSpec(memory_space=pltpu.SMEM),
            ],
            out_specs=[pl.BlockSpec(memory_space=pltpu.VMEM)] * 2,
            scratch_shapes=[
                pltpu.VMEM((2, k, cx + 2, cy + 2 * PAD, nz), jnp.float32),
                pltpu.VMEM((2, 2, k, cx, nz), jnp.float32),
                pltpu.VMEM((2, 2, k, cx, nz), jnp.float32),
                pltpu.VMEM((slots, 8, capacity), jnp.float32),
                pltpu.VMEM((slots, 8, capacity), jnp.float32),
                pltpu.VMEM((k * cx * cy, 2 * nz), jnp.bfloat16),
                pltpu.VMEM((2, cx * cy, capacity), jnp.bfloat16),
                pltpu.VMEM((cx * cy, nz), jnp.float32),
                sem, sem((2, 2, cy // CHUNK)), sem((2, 2, cy // CHUNK)), sem((2, 2)), sem((2, 2)),
                sem((slots,)), sem((slots,)),
            ],
            compiler_params=pltpu.CompilerParams(
                collective_id=0, has_side_effects=True, vmem_limit_bytes=40 * 1024 * 1024
            ),
            name="fire_step",
        )(fields, embers.reshape(7 * slots, 1, capacity), counts)
        return advanced, landed.reshape(4, 1, 1, slots, capacity)

    placed = (
        P(None, "down", "cross", None),
        P(None, "down", "cross", None, None),
        P("down", "cross", None),
    )
    return jax.shard_map(
        local,
        mesh=mesh,
        in_specs=placed,
        out_specs=(P(None, "down", "cross", None), P(None, "down", "cross", None, None)),
        check_vma=False,
    )
```

```python
import functools

import jax
import jax.numpy as jnp
from jax import lax
from jax.experimental import pallas as pl
from jax.experimental.pallas import tpu as pltpu
from jax.sharding import PartitionSpec as P

STEPS = 6
HORIZONTAL_MIX = 0.1
VERTICAL_MIX = 0.1
ADVECTION = 0.25
DRAG_RATE = 0.6
BURN_RATE = 0.5
HEAT_YIELD = 4.0
DESTINATIONS = ((1, -1), (1, 0), (1, 1), (2, -1), (2, 0), (2, 1))
PAD = 8
CHUNK = 32
MESH = pl.DeviceIdType.MESH


def halves(x):
    high = x.astype(jnp.bfloat16)
    return high, (x - high.astype(jnp.float32)).astype(jnp.bfloat16)


def tent(position, cells):
    centres = lax.broadcasted_iota(jnp.int32, (cells, position.shape[1]), 0).astype(jnp.float32) + 0.5
    return jnp.maximum(0.0, 1.0 - jnp.abs(position - centres))


def kernel(
    nd, nc, fields_ref, embers_ref, counts_ref, advanced_ref, landed_ref,
    state, ysend, yrecv, esend, erecv, split, spread, deposit, result,
    in_sem, out_sem, edge_sem, x_send, x_recv, y_send, y_recv, e_send, e_recv,
):
    fields, cx, cy, nz = fields_ref.shape
    slots, capacity = len(DESTINATIONS), embers_ref.shape[2]
    d = lax.axis_index("down")
    c = lax.axis_index("cross")
    rows = pl.ds(PAD, cy)
    parts = cy // CHUNK
    cells = cx * cy

    def inside(a, b):
        return (d + a >= 0) & (d + a < nd) & (c + b >= 0) & (c + b < nc)

    loading = pltpu.make_async_copy(fields_ref, state.at[0, :, pl.ds(1, cx), rows], in_sem)
    loading.start()

    zero_row = jnp.zeros((cy, nz), jnp.float32)
    for b in range(2):
        for k in range(fields):
            state[b, k, 0, PAD:PAD + cy, :] = zero_row
            state[b, k, cx + 1, PAD:PAD + cy, :] = zero_row
    yrecv[...] = jnp.zeros(yrecv.shape, jnp.float32)
    erecv[...] = jnp.zeros(erecv.shape, jnp.float32)

    barrier = pltpu.get_barrier_semaphore()
    peers = [(a, b) for a in (-2, -1, 1, 2) for b in (-1, 0, 1)] + [(0, -1), (0, 1)]
    present = 0
    for a, b in peers:
        there = inside(a, b)
        present = present + there.astype(jnp.int32)

        @pl.when(there)
        def _(a=a, b=b):
            pl.semaphore_signal(barrier, inc=1, device_id=(d + a, c + b), device_id_type=MESH)

    lane = lax.broadcasted_iota(jnp.int32, (1, capacity), 1)
    for j in range(slots):
        live = lane < counts_ref[0, 0, j]
        for i in range(7):
            esend[j, i:i + 1, :] = jnp.where(live, embers_ref[i * slots + j], 0.0)
        esend[j, 7:8, :] = jnp.zeros((1, capacity), jnp.float32)

    def x_copy(b, side, part):
        source, target, by = ((cx, 0, 1), (1, cx + 1, -1))[side]
        band = pl.ds(PAD + part * CHUNK, CHUNK)
        return pltpu.make_async_remote_copy(
            src_ref=state.at[b, :, source, band],
            dst_ref=state.at[b, :, target, band],
            send_sem=x_send.at[b, side, part], recv_sem=x_recv.at[b, side, part],
            device_id=(d + by, c), device_id_type=MESH,
        )

    def y_copy(b, side):
        by = (1, -1)[side]
        return pltpu.make_async_remote_copy(
            src_ref=ysend.at[b, side], dst_ref=yrecv.at[b, side],
            send_sem=y_send.at[b, side], recv_sem=y_recv.at[b, side],
            device_id=(d, c + by), device_id_type=MESH,
        )

    def e_copy(j):
        a, b = DESTINATIONS[j]
        return pltpu.make_async_remote_copy(
            src_ref=esend.at[j], dst_ref=erecv.at[j],
            send_sem=e_send.at[j], recv_sem=e_recv.at[j],
            device_id=(d + a, c + b), device_id_type=MESH,
        )

    def each_side(down, from_there, act):
        for side, by in enumerate((1, -1)):
            by = -by if from_there else by

            @pl.when(inside(by, 0) if down else inside(0, by))
            def _(side=side):
                act(side)

    def start_x(b, part):
        each_side(True, False, lambda side: x_copy(b, side, part).start())

    def arrive_x(b, part):
        each_side(True, True, lambda side: x_copy(b, side, part).wait_recv())

    def sent_x(b, part):
        each_side(True, False, lambda side: x_copy(b, side, part).wait_send())

    def sent_y(b):
        each_side(False, False, lambda side: y_copy(b, side).wait_send())

    def start_y(b):
        for k in range(fields):
            for i in range(cx):
                ysend[b, 0, k, i:i + 1, :] = state[b, k, i + 1, PAD + cy - 1:PAD + cy, :]
                ysend[b, 1, k, i:i + 1, :] = state[b, k, i + 1, PAD:PAD + 1, :]
        each_side(False, False, lambda side: y_copy(b, side).start())

    def arrive_y(b):
        each_side(False, True, lambda side: y_copy(b, side).wait_recv())
        for k in range(fields):
            for i in range(cx):
                state[b, k, i + 1, PAD - 1:PAD, :] = yrecv[b, 0, k, i:i + 1, :]
                state[b, k, i + 1, PAD + cy:PAD + cy + 1, :] = yrecv[b, 1, k, i:i + 1, :]

    level = lax.broadcasted_iota(jnp.int32, (CHUNK, nz), 1)
    keep = 1.0 - 4.0 * HORIZONTAL_MIX - 2.0 * VERTICAL_MIX

    def stencil(b, i, part, last):
        for y in (part * CHUNK,):
            here = slice(PAD + y, PAD + y + CHUNK)
            u = state[b, 0, i, here, :] * (0.5 * ADVECTION)
            v = state[b, 1, i, here, :] * (0.5 * ADVECTION)
            for k in range(fields):
                centre = state[b, k, i, here, :]
                eastern = state[b, k, i + 1, here, :]
                western = state[b, k, i - 1, here, :]
                northern = state[b, k, i, PAD + y + 1:PAD + y + 1 + CHUNK, :]
                southern = state[b, k, i, PAD + y - 1:PAD + y - 1 + CHUNK, :]
                upper = jnp.where(level == nz - 1, centre, pltpu.roll(centre, nz - 1, 1))
                lower = jnp.where(level == 0, centre, pltpu.roll(centre, 1, 1))
                new = (
                    keep * centre
                    + HORIZONTAL_MIX * ((eastern + western) + (northern + southern))
                    + VERTICAL_MIX * (upper + lower)
                    - (u * (eastern - western) + v * (northern - southern))
                )
                if not last:
                    state[1 - b, k, i, here, :] = new
                else:
                    if k == 2:
                        new = new + deposit[pl.ds(pl.multiple_of((i - 1) * cy + y, CHUNK), CHUNK), :]
                    result[k, i - 1, y:y + CHUNK, :] = new

    def embers_of(j):
        a, b = DESTINATIONS[j]

        @pl.when(inside(-a, -b))
        def _():
            e_copy(j).wait_recv()

        def part(i):
            return erecv[j, i:i + 1, :]

        wx = tent(part(0) * cx, cx)
        wy = tent(part(1) * cy, cy)
        wz = tent(part(2) * nz, nz)
        for i in range(cx):
            high, low = halves(wx[i:i + 1, :] * wy)
            spread[i * cy:(i + 1) * cy, :] = high
            spread[cells + i * cy:cells + (i + 1) * cy, :] = low
            spread[2 * cells + i * cy:2 * cells + (i + 1) * cy, :] = high
        columns = jnp.dot(split[...], spread[...], preferred_element_type=jnp.float32)
        weighed = jnp.sum(columns.reshape(fields, nz, capacity) * wz[None], axis=1)
        sampled = [weighed[k:k + 1, :] for k in range(fields)]
        ue, ve, mass, heat = part(3), part(4), part(5), part(6)
        burned = mass * BURN_RATE * jax.nn.sigmoid(heat + sampled[2] - sampled[3])
        living = mass > 0.0
        outs = (
            ue + DRAG_RATE * (sampled[0] - ue),
            ve + DRAG_RATE * (sampled[1] - ve),
            heat + DRAG_RATE * (sampled[2] - heat),
            mass - burned,
        )
        for i in range(4):
            landed_ref[i * slots + j] = jnp.where(living, outs[i], 0.0)
        g_high, g_low = halves(wz * (HEAT_YIELD * burned))

        def nt(p, q):
            return lax.dot_general(p, q, (((1,), (1,)), ((), ())), preferred_element_type=jnp.float32)

        both = nt(spread[:cells, :], jnp.concatenate([g_high, g_low], axis=0))
        add = both[:, :nz] + both[:, nz:] + nt(spread[cells:2 * cells, :], g_high)
        deposit[...] = add if j == 0 else deposit[...] + add

    pl.semaphore_wait(barrier, present)
    for j in range(slots):
        @pl.when(inside(*DESTINATIONS[j]))
        def _(j=j):
            e_copy(j).start()
    loading.wait()

    for part in range(parts):
        start_x(0, part)
    start_y(0)
    for k in range(fields):
        at = slice(k * nz, (k + 1) * nz)
        own = state[0, k, 1:cx + 1, PAD:PAD + cy, :].reshape(cells, nz)
        high, low = halves(own.T)
        split[at, :cells] = high
        split[at, cells:2 * cells] = high
        split[at, 2 * cells:] = low

    inner_rows = pl.ds(1, cx - 2)
    inner_out = pltpu.make_async_copy(result.at[:, inner_rows], advanced_ref.at[:, inner_rows], out_sem.at[0])
    for step in range(STEPS):
        b = step % 2
        last = step == STEPS - 1
        embers_of(step)
        arrive_y(b)
        for part in range(parts):
            arrive_x(b, part)
            if step > 0:
                sent_x(1 - b, part)
            stencil(b, 1, part, last)
            stencil(b, cx, part, last)
            if not last:
                start_x(1 - b, part)
            if part == 0:
                def inner(i, carry, b=b, last=last):
                    for part in range(parts):
                        stencil(b, i, part, last)
                    return carry

                lax.fori_loop(2, cx, inner, 0)
                if last:
                    inner_out.start()
        if step > 0:
            sent_y(1 - b)
        if not last:
            start_y(1 - b)
    outer_out = []
    for side, i in enumerate((0, cx - 1)):
        outer_out.append(pltpu.make_async_copy(result.at[:, i], advanced_ref.at[:, i], edge_sem.at[side]))
        outer_out[side].start()
    for part in range(parts):
        sent_x((STEPS - 1) % 2, part)
    sent_y((STEPS - 1) % 2)
    for j in range(slots):
        @pl.when(inside(*DESTINATIONS[j]))
        def _(j=j):
            e_copy(j).wait_send()

    inner_out.wait()
    for copy in outer_out:
        copy.wait()

def solution(mesh):
    nd, nc = mesh.shape["down"], mesh.shape["cross"]

    def local(fields, embers, counts):
        k, cx, cy, nz = fields.shape
        slots, capacity = embers.shape[3:]
        sem = pltpu.SemaphoreType.DMA
        advanced, landed = pl.pallas_call(
            functools.partial(kernel, nd, nc),
            out_shape=(
                jax.ShapeDtypeStruct(fields.shape, jnp.float32),
                jax.ShapeDtypeStruct((4 * slots, 1, capacity), jnp.float32),
            ),
            in_specs=[
                pl.BlockSpec(memory_space=pltpu.HBM),
                pl.BlockSpec(memory_space=pltpu.VMEM),
                pl.BlockSpec(memory_space=pltpu.SMEM),
            ],
            out_specs=[pl.BlockSpec(memory_space=pltpu.HBM), pl.BlockSpec(memory_space=pltpu.VMEM)],
            scratch_shapes=[
                pltpu.VMEM((2, k, cx + 2, cy + 2 * PAD, nz), jnp.float32),
                pltpu.VMEM((2, 2, k, cx, nz), jnp.float32),
                pltpu.VMEM((2, 2, k, cx, nz), jnp.float32),
                pltpu.VMEM((slots, 8, capacity), jnp.float32),
                pltpu.VMEM((slots, 8, capacity), jnp.float32),
                pltpu.VMEM((k * nz, 3 * cx * cy), jnp.bfloat16),
                pltpu.VMEM((3 * cx * cy, capacity), jnp.bfloat16),
                pltpu.VMEM((cx * cy, nz), jnp.float32),
                pltpu.VMEM(fields.shape, jnp.float32),
                sem, sem((1,)), sem((2,)), sem((2, 2, cy // CHUNK)), sem((2, 2, cy // CHUNK)), sem((2, 2)), sem((2, 2)),
                sem((slots,)), sem((slots,)),
            ],
            compiler_params=pltpu.CompilerParams(
                collective_id=0, has_side_effects=True, vmem_limit_bytes=60 * 1024 * 1024
            ),
            name="fire_step",
        )(fields, embers.reshape(7 * slots, 1, capacity), counts)
        return advanced, landed.reshape(4, 1, 1, slots, capacity)

    placed = (
        P(None, "down", "cross", None),
        P(None, "down", "cross", None, None),
        P("down", "cross", None),
    )
    return jax.shard_map(
        local,
        mesh=mesh,
        in_specs=placed,
        out_specs=(P(None, "down", "cross", None), P(None, "down", "cross", None, None)),
        check_vma=False,
    )
```

```python
import functools

import jax
import jax.numpy as jnp
from jax import lax
from jax.experimental import pallas as pl
from jax.experimental.pallas import tpu as pltpu
from jax.sharding import PartitionSpec as P

STEPS = 6
HORIZONTAL_MIX = 0.1
VERTICAL_MIX = 0.1
ADVECTION = 0.25
DRAG_RATE = 0.6
BURN_RATE = 0.5
HEAT_YIELD = 4.0
DESTINATIONS = ((1, -1), (1, 0), (1, 1), (2, -1), (2, 0), (2, 1))
PAD = 8
CHUNK = 32
BAND = 8
INNER = 24
MESH = pl.DeviceIdType.MESH


def halves(x):
    high = x.astype(jnp.bfloat16)
    return high, (x - high.astype(jnp.float32)).astype(jnp.bfloat16)


def tent(position, cells):
    centres = lax.broadcasted_iota(jnp.int32, (cells, position.shape[1]), 0).astype(jnp.float32) + 0.5
    return jnp.maximum(0.0, 1.0 - jnp.abs(position - centres))


def kernel(
    nd, nc, fields_ref, embers_in, counts_in, advanced_ref, landed_ref, embers_ref, counts_ref,
    state, ysend, yrecv, esend, erecv, split, spread, deposit,
    in_sem, embers_sem, counts_sem, x_send, x_recv, y_send, y_recv, e_send, e_recv,
):
    fields, cx, cy, nz = fields_ref.shape
    slots, capacity = len(DESTINATIONS), embers_ref.shape[2]
    d = lax.axis_index("down")
    c = lax.axis_index("cross")
    rows = pl.ds(PAD, cy)
    parts = cy // CHUNK
    cells = cx * cy

    def inside(a, b):
        return (d + a >= 0) & (d + a < nd) & (c + b >= 0) & (c + b < nc)

    loading = pltpu.make_async_copy(fields_ref, state.at[0, :, pl.ds(1, cx), rows], in_sem)
    loading.start()
    loading_embers = pltpu.make_async_copy(embers_in, embers_ref, embers_sem)
    loading_embers.start()
    loading_counts = pltpu.make_async_copy(counts_in, counts_ref, counts_sem)
    loading_counts.start()

    zero_row = jnp.zeros((cy, nz), jnp.float32)
    for b in range(2):
        for k in range(fields):
            state[b, k, 0, PAD:PAD + cy, :] = zero_row
            state[b, k, cx + 1, PAD:PAD + cy, :] = zero_row
    yrecv[...] = jnp.zeros(yrecv.shape, jnp.float32)
    erecv[...] = jnp.zeros(erecv.shape, jnp.float32)

    barrier = pltpu.get_barrier_semaphore()
    peers = [(a, b) for a in (-2, -1, 1, 2) for b in (-1, 0, 1)] + [(0, -1), (0, 1)]
    present = 0
    for a, b in peers:
        there = inside(a, b)
        present = present + there.astype(jnp.int32)

        @pl.when(there)
        def _(a=a, b=b):
            pl.semaphore_signal(barrier, inc=1, device_id=(d + a, c + b), device_id_type=MESH)

    loading_counts.wait()
    loading_embers.wait()
    lane = lax.broadcasted_iota(jnp.int32, (1, capacity), 1)
    for j in range(slots):
        live = lane < counts_ref[0, 0, j]
        for i in range(7):
            esend[j, i:i + 1, :] = jnp.where(live, embers_ref[i * slots + j], 0.0)
        esend[j, 7:8, :] = jnp.zeros((1, capacity), jnp.float32)

    def x_copy(b, side, part):
        source, target, by = ((cx, 0, 1), (1, cx + 1, -1))[side]
        band = pl.ds(PAD + part * CHUNK, CHUNK)
        return pltpu.make_async_remote_copy(
            src_ref=state.at[b, :, source, band],
            dst_ref=state.at[b, :, target, band],
            send_sem=x_send.at[b, side, part], recv_sem=x_recv.at[b, side, part],
            device_id=(d + by, c), device_id_type=MESH,
        )

    def y_copy(b, side):
        by = (1, -1)[side]
        return pltpu.make_async_remote_copy(
            src_ref=ysend.at[b, side], dst_ref=yrecv.at[b, side],
            send_sem=y_send.at[b, side], recv_sem=y_recv.at[b, side],
            device_id=(d, c + by), device_id_type=MESH,
        )

    def e_copy(j):
        a, b = DESTINATIONS[j]
        return pltpu.make_async_remote_copy(
            src_ref=esend.at[j], dst_ref=erecv.at[j],
            send_sem=e_send.at[j], recv_sem=e_recv.at[j],
            device_id=(d + a, c + b), device_id_type=MESH,
        )

    def each_side(down, from_there, act):
        for side, by in enumerate((1, -1)):
            by = -by if from_there else by

            @pl.when(inside(by, 0) if down else inside(0, by))
            def _(side=side):
                act(side)

    def start_x(b, part):
        each_side(True, False, lambda side: x_copy(b, side, part).start())

    def arrive_x(b, part):
        each_side(True, True, lambda side: x_copy(b, side, part).wait_recv())

    def sent_x(b, part):
        each_side(True, False, lambda side: x_copy(b, side, part).wait_send())

    def sent_y(b):
        each_side(False, False, lambda side: y_copy(b, side).wait_send())

    def start_y(b):
        for k in range(fields):
            for i in range(cx):
                ysend[b, 0, k, i:i + 1, :] = state[b, k, i + 1, PAD + cy - 1:PAD + cy, :]
                ysend[b, 1, k, i:i + 1, :] = state[b, k, i + 1, PAD:PAD + 1, :]
        each_side(False, False, lambda side: y_copy(b, side).start())

    def arrive_y(b):
        each_side(False, True, lambda side: y_copy(b, side).wait_recv())
        for k in range(fields):
            for i in range(cx):
                state[b, k, i + 1, PAD - 1:PAD, :] = yrecv[b, 0, k, i:i + 1, :]
                state[b, k, i + 1, PAD + cy:PAD + cy + 1, :] = yrecv[b, 1, k, i:i + 1, :]

    level = lax.broadcasted_iota(jnp.int32, (CHUNK, nz), 1)
    keep = 1.0 - 4.0 * HORIZONTAL_MIX - 2.0 * VERTICAL_MIX

    def stencil(b, i, y, span, last):
        here = slice(PAD + y, PAD + y + span)
        u = state[b, 0, i, here, :] * (0.5 * ADVECTION)
        v = state[b, 1, i, here, :] * (0.5 * ADVECTION)
        for k in range(fields):
            centre = state[b, k, i, here, :]
            eastern = state[b, k, i + 1, here, :]
            western = state[b, k, i - 1, here, :]
            northern = state[b, k, i, PAD + y + 1:PAD + y + 1 + span, :]
            southern = state[b, k, i, PAD + y - 1:PAD + y - 1 + span, :]
            upper = jnp.where(level[:span] == nz - 1, centre, pltpu.roll(centre, nz - 1, 1))
            lower = jnp.where(level[:span] == 0, centre, pltpu.roll(centre, 1, 1))
            new = (
                keep * centre
                + HORIZONTAL_MIX * ((eastern + western) + (northern + southern))
                + VERTICAL_MIX * (upper + lower)
                - (u * (eastern - western) + v * (northern - southern))
            )
            if not last:
                state[1 - b, k, i, here, :] = new
            else:
                if k == 2:
                    new = new + deposit[pl.ds(pl.multiple_of((i - 1) * cy + y, BAND), span), :]
                advanced_ref[k, i - 1, y:y + span, :] = new

    def embers_of(j):
        a, b = DESTINATIONS[j]

        @pl.when(inside(-a, -b))
        def _():
            e_copy(j).wait_recv()

        def part(i):
            return erecv[j, i:i + 1, :]

        wx = tent(part(0) * cx, cx)
        wy = tent(part(1) * cy, cy)
        wz = tent(part(2) * nz, nz)
        for i in range(cx):
            high, low = halves(wx[i:i + 1, :] * wy)
            spread[i * cy:(i + 1) * cy, :] = high
            spread[cells + i * cy:cells + (i + 1) * cy, :] = low
            spread[2 * cells + i * cy:2 * cells + (i + 1) * cy, :] = high
        columns = jnp.dot(split[...], spread[...], preferred_element_type=jnp.float32)
        weighed = jnp.sum(columns.reshape(fields, nz, capacity) * wz[None], axis=1)
        sampled = [weighed[k:k + 1, :] for k in range(fields)]
        ue, ve, mass, heat = part(3), part(4), part(5), part(6)
        burned = mass * BURN_RATE * jax.nn.sigmoid(heat + sampled[2] - sampled[3])
        living = mass > 0.0
        outs = (
            ue + DRAG_RATE * (sampled[0] - ue),
            ve + DRAG_RATE * (sampled[1] - ve),
            heat + DRAG_RATE * (sampled[2] - heat),
            mass - burned,
        )
        for i in range(4):
            landed_ref[i * slots + j] = jnp.where(living, outs[i], 0.0)
        g_high, g_low = halves(wz * (HEAT_YIELD * burned))

        def nt(p, q):
            return lax.dot_general(p, q, (((1,), (1,)), ((), ())), preferred_element_type=jnp.float32)

        both = nt(spread[:cells, :], jnp.concatenate([g_high, g_low], axis=0))
        add = both[:, :nz] + both[:, nz:] + nt(spread[cells:2 * cells, :], g_high)
        deposit[...] = add if j == 0 else deposit[...] + add

    pl.semaphore_wait(barrier, present)
    for j in range(slots):
        @pl.when(inside(*DESTINATIONS[j]))
        def _(j=j):
            e_copy(j).start()
    loading.wait()

    for part in range(parts):
        start_x(0, part)
    start_y(0)
    for k in range(fields):
        at = slice(k * nz, (k + 1) * nz)
        own = state[0, k, 1:cx + 1, PAD:PAD + cy, :].reshape(cells, nz)
        high, low = halves(own.T)
        split[at, :cells] = high
        split[at, cells:2 * cells] = high
        split[at, 2 * cells:] = low

    for step in range(STEPS):
        b = step % 2
        last = step == STEPS - 1
        embers_of(step)
        arrive_y(b)
        for part in range(parts):
            arrive_x(b, part)
            if step > 0:
                sent_x(1 - b, part)
            stencil(b, 1, part * CHUNK, CHUNK, last)
            stencil(b, cx, part * CHUNK, CHUNK, last)
            if not last:
                start_x(1 - b, part)
        for i in range(2, cx):
            stencil(b, i, 0, BAND, last)
            stencil(b, i, cy - BAND, BAND, last)
        if step > 0:
            sent_y(1 - b)
        if not last:
            start_y(1 - b)

        def inner(i, carry, b=b, last=last):
            for y in range(BAND, cy - BAND, INNER):
                stencil(b, i, y, INNER, last)
            return carry

        lax.fori_loop(2, cx, inner, 0)
    for part in range(parts):
        sent_x((STEPS - 1) % 2, part)
    sent_y((STEPS - 1) % 2)
    for j in range(slots):
        @pl.when(inside(*DESTINATIONS[j]))
        def _(j=j):
            e_copy(j).wait_send()

def store(advanced_ref, landed_ref, advanced_out, landed_out, advanced_sem, landed_sem):
    copies = (
        pltpu.make_async_copy(advanced_ref, advanced_out, advanced_sem),
        pltpu.make_async_copy(landed_ref, landed_out, landed_sem),
    )
    for copy in copies:
        copy.start()
    for copy in copies:
        copy.wait()


def solution(mesh):
    nd, nc = mesh.shape["down"], mesh.shape["cross"]

    def local(fields, embers, counts):
        k, cx, cy, nz = fields.shape
        slots, capacity = embers.shape[3:]
        arguments = (fields, embers.reshape(7 * slots, 1, capacity), counts)
        sem = pltpu.SemaphoreType.DMA
        advanced, landed = pl.pallas_call(
            functools.partial(kernel, nd, nc),
            out_shape=(
                pltpu.VMEM(fields.shape, jnp.float32),
                pltpu.VMEM((4 * slots, 1, capacity), jnp.float32),
            ),
            in_specs=[
                pl.BlockSpec(memory_space=pltpu.HBM),
            ] * 3,
            out_specs=[pl.BlockSpec(memory_space=pltpu.VMEM)] * 2,
            scratch_shapes=[
                pltpu.VMEM((7 * slots, 1, capacity), jnp.float32),
                pltpu.SMEM(counts.shape, jnp.int32),
                pltpu.VMEM((2, k, cx + 2, cy + 2 * PAD, nz), jnp.float32),
                pltpu.VMEM((2, 2, k, cx, nz), jnp.float32),
                pltpu.VMEM((2, 2, k, cx, nz), jnp.float32),
                pltpu.VMEM((slots, 8, capacity), jnp.float32),
                pltpu.VMEM((slots, 8, capacity), jnp.float32),
                pltpu.VMEM((k * nz, 3 * cx * cy), jnp.bfloat16),
                pltpu.VMEM((3 * cx * cy, capacity), jnp.bfloat16),
                pltpu.VMEM((cx * cy, nz), jnp.float32),
                sem, sem, sem, sem((2, 2, cy // CHUNK)), sem((2, 2, cy // CHUNK)), sem((2, 2)), sem((2, 2)),
                sem((slots,)), sem((slots,)),
            ],
            compiler_params=pltpu.CompilerParams(
                collective_id=0, has_side_effects=True, vmem_limit_bytes=40 * 1024 * 1024
            ),
            name="fire_step",
        )(*[pltpu.with_memory_space_constraint(x, pltpu.HBM) for x in arguments])
        advanced, landed = pl.pallas_call(
            store,
            out_shape=(
                jax.ShapeDtypeStruct(advanced.shape, jnp.float32),
                jax.ShapeDtypeStruct(landed.shape, jnp.float32),
            ),
            in_specs=[pl.BlockSpec(memory_space=pl.ANY)] * 2,
            out_specs=[pl.BlockSpec(memory_space=pltpu.HBM)] * 2,
            scratch_shapes=[sem, sem],
            name="store_results",
        )(advanced, landed)
        return advanced, landed.reshape(4, 1, 1, slots, capacity)

    placed = (
        P(None, "down", "cross", None),
        P(None, "down", "cross", None, None),
        P("down", "cross", None),
    )
    return jax.shard_map(
        local,
        mesh=mesh,
        in_specs=placed,
        out_specs=(P(None, "down", "cross", None), P(None, "down", "cross", None, None)),
        check_vma=False,
    )
```

```python
import functools

import jax
import jax.numpy as jnp
from jax import lax
from jax.experimental import pallas as pl
from jax.experimental.pallas import tpu as pltpu
from jax.sharding import PartitionSpec as P

STEPS = 6
HORIZONTAL_MIX = 0.1
VERTICAL_MIX = 0.1
ADVECTION = 0.25
DRAG_RATE = 0.6
BURN_RATE = 0.5
HEAT_YIELD = 4.0
DESTINATIONS = ((1, -1), (1, 0), (1, 1), (2, -1), (2, 0), (2, 1))
PAD = 8
OUTER = 16
BAND = 8
INNER = 24
MESH = pl.DeviceIdType.MESH


def halves(x):
    high = x.astype(jnp.bfloat16)
    return high, (x - high.astype(jnp.float32)).astype(jnp.bfloat16)


def tent(position, cells):
    centres = lax.broadcasted_iota(jnp.int32, (cells, position.shape[1]), 0).astype(jnp.float32) + 0.5
    return jnp.maximum(0.0, 1.0 - jnp.abs(position - centres))


def kernel(
    nd, nc, fields_ref, embers_in, counts_in, advanced_ref, landed_ref, embers_ref, counts_ref,
    state, ysend, yrecv, esend, erecv, split, spread, deposit,
    in_sem, embers_sem, counts_sem, x_send, x_recv, y_send, y_recv, e_send, e_recv,
):
    fields, cx, cy, nz = fields_ref.shape
    slots, capacity = len(DESTINATIONS), embers_ref.shape[2]
    d = lax.axis_index("down")
    c = lax.axis_index("cross")
    rows = pl.ds(PAD, cy)
    segments = ((0, OUTER), (cy - OUTER, OUTER), (OUTER, cy - 2 * OUTER))
    cells = cx * cy

    def inside(a, b):
        return (d + a >= 0) & (d + a < nd) & (c + b >= 0) & (c + b < nc)

    loading = pltpu.make_async_copy(fields_ref, state.at[0, :, pl.ds(1, cx), rows], in_sem)
    loading.start()
    loading_embers = pltpu.make_async_copy(embers_in, embers_ref, embers_sem)
    loading_embers.start()
    loading_counts = pltpu.make_async_copy(counts_in, counts_ref, counts_sem)
    loading_counts.start()

    zero_row = jnp.zeros((cy, nz), jnp.float32)
    for b in range(2):
        for k in range(fields):
            state[b, k, 0, PAD:PAD + cy, :] = zero_row
            state[b, k, cx + 1, PAD:PAD + cy, :] = zero_row
    yrecv[...] = jnp.zeros(yrecv.shape, jnp.float32)
    erecv[...] = jnp.zeros(erecv.shape, jnp.float32)

    barrier = pltpu.get_barrier_semaphore()
    peers = [(a, b) for a in (-2, -1, 1, 2) for b in (-1, 0, 1)] + [(0, -1), (0, 1)]
    present = 0
    for a, b in peers:
        there = inside(a, b)
        present = present + there.astype(jnp.int32)

        @pl.when(there)
        def _(a=a, b=b):
            pl.semaphore_signal(barrier, inc=1, device_id=(d + a, c + b), device_id_type=MESH)

    loading_counts.wait()
    loading_embers.wait()
    lane = lax.broadcasted_iota(jnp.int32, (1, capacity), 1)
    for j in range(slots):
        live = lane < counts_ref[0, 0, j]
        for i in range(7):
            esend[j, i:i + 1, :] = jnp.where(live, embers_ref[i * slots + j], 0.0)
        esend[j, 7:8, :] = jnp.zeros((1, capacity), jnp.float32)

    def x_copy(b, side, part):
        source, target, by = ((cx, 0, 1), (1, cx + 1, -1))[side]
        band = pl.ds(PAD + segments[part][0], segments[part][1])
        return pltpu.make_async_remote_copy(
            src_ref=state.at[b, :, source, band],
            dst_ref=state.at[b, :, target, band],
            send_sem=x_send.at[b, side, part], recv_sem=x_recv.at[b, side, part],
            device_id=(d + by, c), device_id_type=MESH,
        )

    def y_copy(b, side):
        by = (1, -1)[side]
        return pltpu.make_async_remote_copy(
            src_ref=ysend.at[b, side], dst_ref=yrecv.at[b, side],
            send_sem=y_send.at[b, side], recv_sem=y_recv.at[b, side],
            device_id=(d, c + by), device_id_type=MESH,
        )

    def e_copy(j):
        a, b = DESTINATIONS[j]
        return pltpu.make_async_remote_copy(
            src_ref=esend.at[j], dst_ref=erecv.at[j],
            send_sem=e_send.at[j], recv_sem=e_recv.at[j],
            device_id=(d + a, c + b), device_id_type=MESH,
        )

    def each_side(down, from_there, act):
        for side, by in enumerate((1, -1)):
            by = -by if from_there else by

            @pl.when(inside(by, 0) if down else inside(0, by))
            def _(side=side):
                act(side)

    def start_x(b, part):
        each_side(True, False, lambda side: x_copy(b, side, part).start())

    def arrive_x(b, part):
        each_side(True, True, lambda side: x_copy(b, side, part).wait_recv())

    def sent_x(b, part):
        each_side(True, False, lambda side: x_copy(b, side, part).wait_send())

    def sent_y(b):
        each_side(False, False, lambda side: y_copy(b, side).wait_send())

    def start_y(b):
        for k in range(fields):
            for i in range(cx):
                ysend[b, 0, k, i:i + 1, :] = state[b, k, i + 1, PAD + cy - 1:PAD + cy, :]
                ysend[b, 1, k, i:i + 1, :] = state[b, k, i + 1, PAD:PAD + 1, :]
        each_side(False, False, lambda side: y_copy(b, side).start())

    def arrive_y(b):
        each_side(False, True, lambda side: y_copy(b, side).wait_recv())
        for k in range(fields):
            for i in range(cx):
                state[b, k, i + 1, PAD - 1:PAD, :] = yrecv[b, 0, k, i:i + 1, :]
                state[b, k, i + 1, PAD + cy:PAD + cy + 1, :] = yrecv[b, 1, k, i:i + 1, :]

    level = lax.broadcasted_iota(jnp.int32, (32, nz), 1)
    keep = 1.0 - 4.0 * HORIZONTAL_MIX - 2.0 * VERTICAL_MIX

    def stencil(b, i, y, span, last):
        here = slice(PAD + y, PAD + y + span)
        u = state[b, 0, i, here, :] * (0.5 * ADVECTION)
        v = state[b, 1, i, here, :] * (0.5 * ADVECTION)
        for k in range(fields):
            centre = state[b, k, i, here, :]
            eastern = state[b, k, i + 1, here, :]
            western = state[b, k, i - 1, here, :]
            northern = state[b, k, i, PAD + y + 1:PAD + y + 1 + span, :]
            southern = state[b, k, i, PAD + y - 1:PAD + y - 1 + span, :]
            upper = jnp.where(level[:span] == nz - 1, centre, pltpu.roll(centre, nz - 1, 1))
            lower = jnp.where(level[:span] == 0, centre, pltpu.roll(centre, 1, 1))
            new = (
                keep * centre
                + HORIZONTAL_MIX * ((eastern + western) + (northern + southern))
                + VERTICAL_MIX * (upper + lower)
                - (u * (eastern - western) + v * (northern - southern))
            )
            if not last:
                state[1 - b, k, i, here, :] = new
            else:
                if k == 2:
                    new = new + deposit[pl.ds(pl.multiple_of((i - 1) * cy + y, BAND), span), :]
                advanced_ref[k, i - 1, y:y + span, :] = new

    def embers_of(j):
        a, b = DESTINATIONS[j]

        @pl.when(inside(-a, -b))
        def _():
            e_copy(j).wait_recv()

        def part(i):
            return erecv[j, i:i + 1, :]

        wx = tent(part(0) * cx, cx)
        wy = tent(part(1) * cy, cy)
        wz = tent(part(2) * nz, nz)
        for i in range(cx):
            high, low = halves(wx[i:i + 1, :] * wy)
            spread[i * cy:(i + 1) * cy, :] = high
            spread[cells + i * cy:cells + (i + 1) * cy, :] = low
            spread[2 * cells + i * cy:2 * cells + (i + 1) * cy, :] = high
        columns = jnp.dot(split[...], spread[...], preferred_element_type=jnp.float32)
        weighed = jnp.sum(columns.reshape(fields, nz, capacity) * wz[None], axis=1)
        sampled = [weighed[k:k + 1, :] for k in range(fields)]
        ue, ve, mass, heat = part(3), part(4), part(5), part(6)
        burned = mass * BURN_RATE * jax.nn.sigmoid(heat + sampled[2] - sampled[3])
        living = mass > 0.0
        outs = (
            ue + DRAG_RATE * (sampled[0] - ue),
            ve + DRAG_RATE * (sampled[1] - ve),
            heat + DRAG_RATE * (sampled[2] - heat),
            mass - burned,
        )
        for i in range(4):
            landed_ref[i * slots + j] = jnp.where(living, outs[i], 0.0)
        g_high, g_low = halves(wz * (HEAT_YIELD * burned))

        def nt(p, q):
            return lax.dot_general(p, q, (((1,), (1,)), ((), ())), preferred_element_type=jnp.float32)

        both = nt(spread[:cells, :], jnp.concatenate([g_high, g_low], axis=0))
        add = both[:, :nz] + both[:, nz:] + nt(spread[cells:2 * cells, :], g_high)
        deposit[...] = add if j == 0 else deposit[...] + add

    pl.semaphore_wait(barrier, present)
    for j in range(slots):
        @pl.when(inside(*DESTINATIONS[j]))
        def _(j=j):
            e_copy(j).start()
    loading.wait()

    start_x(0, 0)
    start_x(0, 1)
    start_y(0)
    start_x(0, 2)

    for step in range(STEPS):
        b = step % 2
        last = step == STEPS - 1

        def edges(part, b=b, step=step, last=last):
            arrive_x(b, part)
            if step > 0:
                sent_x(1 - b, part)
            y, span = segments[part]
            stencil(b, 1, y, span, last)
            stencil(b, cx, y, span, last)
            if not last:
                start_x(1 - b, part)

        def inner(i, carry, b=b, last=last):
            for y in range(BAND, cy - BAND, INNER):
                stencil(b, i, y, INNER, last)
            return carry

        if last:
            embers_of(step)
        arrive_y(b)
        edges(0)
        edges(1)
        for i in range(2, cx):
            stencil(b, i, 0, BAND, last)
            stencil(b, i, cy - BAND, BAND, last)
        if step > 0:
            sent_y(1 - b)
        if not last:
            start_y(1 - b)
        lax.fori_loop(2, cx, inner, 0)
        if step == 0:
            for k in range(fields):
                at = slice(k * nz, (k + 1) * nz)
                own = state[0, k, 1:cx + 1, PAD:PAD + cy, :].reshape(cells, nz)
                high, low = halves(own.T)
                split[at, :cells] = high
                split[at, cells:2 * cells] = high
                split[at, 2 * cells:] = low
        if not last:
            embers_of(step)
        edges(2)
    for part in range(len(segments)):
        sent_x((STEPS - 1) % 2, part)
    sent_y((STEPS - 1) % 2)
    for j in range(slots):
        @pl.when(inside(*DESTINATIONS[j]))
        def _(j=j):
            e_copy(j).wait_send()

def solution(mesh):
    nd, nc = mesh.shape["down"], mesh.shape["cross"]

    def local(fields, embers, counts):
        k, cx, cy, nz = fields.shape
        slots, capacity = embers.shape[3:]
        arguments = (fields, embers.reshape(7 * slots, 1, capacity), counts)
        sem = pltpu.SemaphoreType.DMA
        advanced, landed = pl.pallas_call(
            functools.partial(kernel, nd, nc),
            out_shape=(
                pltpu.VMEM(fields.shape, jnp.float32),
                pltpu.VMEM((4 * slots, 1, capacity), jnp.float32),
            ),
            in_specs=[
                pl.BlockSpec(memory_space=pltpu.HBM),
            ] * 3,
            out_specs=[pl.BlockSpec(memory_space=pltpu.VMEM)] * 2,
            scratch_shapes=[
                pltpu.VMEM((7 * slots, 1, capacity), jnp.float32),
                pltpu.SMEM(counts.shape, jnp.int32),
                pltpu.VMEM((2, k, cx + 2, cy + 2 * PAD, nz), jnp.float32),
                pltpu.VMEM((2, 2, k, cx, nz), jnp.float32),
                pltpu.VMEM((2, 2, k, cx, nz), jnp.float32),
                pltpu.VMEM((slots, 8, capacity), jnp.float32),
                pltpu.VMEM((slots, 8, capacity), jnp.float32),
                pltpu.VMEM((k * nz, 3 * cx * cy), jnp.bfloat16),
                pltpu.VMEM((3 * cx * cy, capacity), jnp.bfloat16),
                pltpu.VMEM((cx * cy, nz), jnp.float32),
                sem, sem, sem, sem((2, 2, 3)), sem((2, 2, 3)), sem((2, 2)), sem((2, 2)),
                sem((slots,)), sem((slots,)),
            ],
            compiler_params=pltpu.CompilerParams(
                collective_id=0, has_side_effects=True, vmem_limit_bytes=40 * 1024 * 1024
            ),
            name="fire_step",
        )(*[pltpu.with_memory_space_constraint(x, pltpu.HBM) for x in arguments])
        return advanced, landed.reshape(4, 1, 1, slots, capacity)

    placed = (
        P(None, "down", "cross", None),
        P(None, "down", "cross", None, None),
        P("down", "cross", None),
    )
    return jax.shard_map(
        local,
        mesh=mesh,
        in_specs=placed,
        out_specs=(P(None, "down", "cross", None), P(None, "down", "cross", None, None)),
        check_vma=False,
    )
```

```python
import functools

import jax
import jax.numpy as jnp
from jax import lax
from jax.experimental import pallas as pl
from jax.experimental.pallas import tpu as pltpu
from jax.sharding import PartitionSpec as P

STEPS = 6
HORIZONTAL_MIX = 0.1
VERTICAL_MIX = 0.1
ADVECTION = 0.25
DRAG_RATE = 0.6
BURN_RATE = 0.5
HEAT_YIELD = 4.0
DESTINATIONS = ((1, -1), (1, 0), (1, 1), (2, -1), (2, 0), (2, 1))
PAD = 8
OUTER = 16
BAND = 8
INNER = 24
MESH = pl.DeviceIdType.MESH


def halves(x):
    high = x.astype(jnp.bfloat16)
    return high, (x - high.astype(jnp.float32)).astype(jnp.bfloat16)


def tent(position, cells):
    centres = lax.broadcasted_iota(jnp.int32, (cells, position.shape[1]), 0).astype(jnp.float32) + 0.5
    return jnp.maximum(0.0, 1.0 - jnp.abs(position - centres))


def kernel(
    nd, nc, fields_ref, embers_in, counts_in, advanced_ref, landed_ref, embers_ref, counts_ref,
    state, ysend, yrecv, esend, erecv, split, spread, deposit,
    in_sem, embers_sem, counts_sem, x_send, x_recv, y_send, y_recv, e_send, e_recv,
):
    fields, cx, cy, nz = fields_ref.shape
    slots, capacity = len(DESTINATIONS), embers_ref.shape[2]
    d = lax.axis_index("down")
    c = lax.axis_index("cross")
    rows = pl.ds(PAD, cy)
    segments = ((0, OUTER), (cy - OUTER, OUTER), (OUTER, cy - 2 * OUTER))
    cells = cx * cy

    def inside(a, b):
        return (d + a >= 0) & (d + a < nd) & (c + b >= 0) & (c + b < nc)

    loading = pltpu.make_async_copy(fields_ref, state.at[0, :, pl.ds(1, cx), rows], in_sem)
    loading.start()
    loading_embers = pltpu.make_async_copy(embers_in, embers_ref, embers_sem)
    loading_embers.start()
    loading_counts = pltpu.make_async_copy(counts_in, counts_ref, counts_sem)
    loading_counts.start()

    zero_row = jnp.zeros((cy, nz), jnp.float32)
    for b in range(2):
        for k in range(fields):
            state[b, k, 0, PAD:PAD + cy, :] = zero_row
            state[b, k, cx + 1, PAD:PAD + cy, :] = zero_row
    yrecv[...] = jnp.zeros(yrecv.shape, jnp.float32)
    erecv[...] = jnp.zeros(erecv.shape, jnp.float32)

    barrier = pltpu.get_barrier_semaphore()
    peers = [(a, b) for a in (-2, -1, 1, 2) for b in (-1, 0, 1)] + [(0, -1), (0, 1)]
    present = 0
    for a, b in peers:
        there = inside(a, b)
        present = present + there.astype(jnp.int32)

        @pl.when(there)
        def _(a=a, b=b):
            pl.semaphore_signal(barrier, inc=1, device_id=(d + a, c + b), device_id_type=MESH)

    loading_counts.wait()
    loading_embers.wait()
    lane = lax.broadcasted_iota(jnp.int32, (1, capacity), 1)
    for j in range(slots):
        live = lane < counts_ref[0, 0, j]
        for i in range(7):
            esend[j, i:i + 1, :] = jnp.where(live, embers_ref[i * slots + j], 0.0)
        esend[j, 7:8, :] = jnp.zeros((1, capacity), jnp.float32)

    def x_copy(b, side, part):
        source, target, by = ((cx, 0, 1), (1, cx + 1, -1))[side]
        band = pl.ds(PAD + segments[part][0], segments[part][1])
        return pltpu.make_async_remote_copy(
            src_ref=state.at[b, :, source, band],
            dst_ref=state.at[b, :, target, band],
            send_sem=x_send.at[b, side, part], recv_sem=x_recv.at[b, side, part],
            device_id=(d + by, c), device_id_type=MESH,
        )

    def y_copy(b, side):
        by = (1, -1)[side]
        return pltpu.make_async_remote_copy(
            src_ref=ysend.at[b, side], dst_ref=yrecv.at[b, side],
            send_sem=y_send.at[b, side], recv_sem=y_recv.at[b, side],
            device_id=(d, c + by), device_id_type=MESH,
        )

    def e_copy(j):
        a, b = DESTINATIONS[j]
        return pltpu.make_async_remote_copy(
            src_ref=esend.at[j], dst_ref=erecv.at[j],
            send_sem=e_send.at[j], recv_sem=e_recv.at[j],
            device_id=(d + a, c + b), device_id_type=MESH,
        )

    def each_side(down, from_there, act):
        for side, by in enumerate((1, -1)):
            by = -by if from_there else by

            @pl.when(inside(by, 0) if down else inside(0, by))
            def _(side=side):
                act(side)

    def start_x(b, part):
        each_side(True, False, lambda side: x_copy(b, side, part).start())

    def arrive_x(b, part):
        each_side(True, True, lambda side: x_copy(b, side, part).wait_recv())

    def sent_x(b, part):
        each_side(True, False, lambda side: x_copy(b, side, part).wait_send())

    def sent_y(b):
        each_side(False, False, lambda side: y_copy(b, side).wait_send())

    def start_y(b):
        for k in range(fields):
            for i in range(cx):
                ysend[b, 0, k, i:i + 1, :] = state[b, k, i + 1, PAD + cy - 1:PAD + cy, :]
                ysend[b, 1, k, i:i + 1, :] = state[b, k, i + 1, PAD:PAD + 1, :]
        each_side(False, False, lambda side: y_copy(b, side).start())

    def arrive_y(b):
        each_side(False, True, lambda side: y_copy(b, side).wait_recv())
        for k in range(fields):
            for i in range(cx):
                state[b, k, i + 1, PAD - 1:PAD, :] = yrecv[b, 0, k, i:i + 1, :]
                state[b, k, i + 1, PAD + cy:PAD + cy + 1, :] = yrecv[b, 1, k, i:i + 1, :]

    level = lax.broadcasted_iota(jnp.int32, (32, nz), 1)
    keep = 1.0 - 4.0 * HORIZONTAL_MIX - 2.0 * VERTICAL_MIX

    def stencil(b, i, y, span, last):
        here = slice(PAD + y, PAD + y + span)
        u = state[b, 0, i, here, :] * (0.5 * ADVECTION)
        v = state[b, 1, i, here, :] * (0.5 * ADVECTION)
        for k in range(fields):
            centre = state[b, k, i, here, :]
            eastern = state[b, k, i + 1, here, :]
            western = state[b, k, i - 1, here, :]
            northern = state[b, k, i, PAD + y + 1:PAD + y + 1 + span, :]
            southern = state[b, k, i, PAD + y - 1:PAD + y - 1 + span, :]
            upper = jnp.where(level[:span] == nz - 1, centre, pltpu.roll(centre, nz - 1, 1))
            lower = jnp.where(level[:span] == 0, centre, pltpu.roll(centre, 1, 1))
            new = (
                keep * centre
                + HORIZONTAL_MIX * ((eastern + western) + (northern + southern))
                + VERTICAL_MIX * (upper + lower)
                - (u * (eastern - western) + v * (northern - southern))
            )
            if not last:
                state[1 - b, k, i, here, :] = new
            else:
                if k == 2:
                    new = new + deposit[pl.ds(pl.multiple_of((i - 1) * cy + y, BAND), span), :]
                advanced_ref[k, i - 1, y:y + span, :] = new

    def embers_of(j):
        a, b = DESTINATIONS[j]

        @pl.when(inside(-a, -b))
        def _():
            e_copy(j).wait_recv()

        def part(i):
            return erecv[j, i:i + 1, :]

        wx = tent(part(0) * cx, cx)
        wy = tent(part(1) * cy, cy)
        wz = tent(part(2) * nz, nz)
        for i in range(cx):
            high, low = halves(wx[i:i + 1, :] * wy)
            spread[i * cy:(i + 1) * cy, :] = high
            spread[cells + i * cy:cells + (i + 1) * cy, :] = low
            spread[2 * cells + i * cy:2 * cells + (i + 1) * cy, :] = high
        columns = jnp.dot(split[...], spread[...], preferred_element_type=jnp.float32)
        weighed = jnp.sum(columns.reshape(fields, nz, capacity) * wz[None], axis=1)
        sampled = [weighed[k:k + 1, :] for k in range(fields)]
        ue, ve, mass, heat = part(3), part(4), part(5), part(6)
        burned = mass * BURN_RATE * jax.nn.sigmoid(heat + sampled[2] - sampled[3])
        living = mass > 0.0
        outs = (
            ue + DRAG_RATE * (sampled[0] - ue),
            ve + DRAG_RATE * (sampled[1] - ve),
            heat + DRAG_RATE * (sampled[2] - heat),
            mass - burned,
        )
        for i in range(4):
            landed_ref[i * slots + j] = jnp.where(living, outs[i], 0.0)
        g_high, g_low = halves(wz * (HEAT_YIELD * burned))

        def nt(p, q):
            return lax.dot_general(p, q, (((1,), (1,)), ((), ())), preferred_element_type=jnp.float32)

        both = nt(spread[:cells, :], jnp.concatenate([g_high, g_low], axis=0))
        add = both[:, :nz] + both[:, nz:] + nt(spread[cells:2 * cells, :], g_high)
        deposit[...] = add if j == 0 else deposit[...] + add

    pl.semaphore_wait(barrier, present)
    for j in range(slots):
        @pl.when(inside(*DESTINATIONS[j]))
        def _(j=j):
            e_copy(j).start()
    loading.wait()

    start_x(0, 0)
    start_x(0, 1)
    start_y(0)
    start_x(0, 2)
    for k in range(fields):
        at = slice(k * nz, (k + 1) * nz)
        own = state[0, k, 1:cx + 1, PAD:PAD + cy, :].reshape(cells, nz)
        high, low = halves(own.T)
        split[at, :cells] = high
        split[at, cells:2 * cells] = high
        split[at, 2 * cells:] = low
    embers_of(0)

    for step in range(STEPS):
        b = step % 2
        last = step == STEPS - 1

        def edges(part, b=b, step=step, last=last):
            arrive_x(b, part)
            if step > 0:
                sent_x(1 - b, part)
            y, span = segments[part]
            stencil(b, 1, y, span, last)
            stencil(b, cx, y, span, last)
            if not last:
                start_x(1 - b, part)

        def inner(i, carry, b=b, last=last):
            for y in range(BAND, cy - BAND, INNER):
                stencil(b, i, y, INNER, last)
            return carry

        arrive_y(b)
        edges(0)
        edges(1)
        for i in range(2, cx):
            stencil(b, i, 0, BAND, last)
            stencil(b, i, cy - BAND, BAND, last)
        if step > 0:
            sent_y(1 - b)
        if not last:
            start_y(1 - b)
        lax.fori_loop(2, cx, inner, 0)
        edges(2)
        if not last:
            embers_of(step + 1)
    for part in range(len(segments)):
        sent_x((STEPS - 1) % 2, part)
    sent_y((STEPS - 1) % 2)
    for j in range(slots):
        @pl.when(inside(*DESTINATIONS[j]))
        def _(j=j):
            e_copy(j).wait_send()

def solution(mesh):
    nd, nc = mesh.shape["down"], mesh.shape["cross"]

    def local(fields, embers, counts):
        k, cx, cy, nz = fields.shape
        slots, capacity = embers.shape[3:]
        arguments = (fields, embers.reshape(7 * slots, 1, capacity), counts)
        sem = pltpu.SemaphoreType.DMA
        advanced, landed = pl.pallas_call(
            functools.partial(kernel, nd, nc),
            out_shape=(
                pltpu.VMEM(fields.shape, jnp.float32),
                pltpu.VMEM((4 * slots, 1, capacity), jnp.float32),
            ),
            in_specs=[
                pl.BlockSpec(memory_space=pltpu.HBM),
            ] * 3,
            out_specs=[pl.BlockSpec(memory_space=pltpu.VMEM)] * 2,
            scratch_shapes=[
                pltpu.VMEM((7 * slots, 1, capacity), jnp.float32),
                pltpu.SMEM(counts.shape, jnp.int32),
                pltpu.VMEM((2, k, cx + 2, cy + 2 * PAD, nz), jnp.float32),
                pltpu.VMEM((2, 2, k, cx, nz), jnp.float32),
                pltpu.VMEM((2, 2, k, cx, nz), jnp.float32),
                pltpu.VMEM((slots, 8, capacity), jnp.float32),
                pltpu.VMEM((slots, 8, capacity), jnp.float32),
                pltpu.VMEM((k * nz, 3 * cx * cy), jnp.bfloat16),
                pltpu.VMEM((3 * cx * cy, capacity), jnp.bfloat16),
                pltpu.VMEM((cx * cy, nz), jnp.float32),
                sem, sem, sem, sem((2, 2, 3)), sem((2, 2, 3)), sem((2, 2)), sem((2, 2)),
                sem((slots,)), sem((slots,)),
            ],
            compiler_params=pltpu.CompilerParams(
                collective_id=0, has_side_effects=True, vmem_limit_bytes=40 * 1024 * 1024
            ),
            name="fire_step",
        )(*[pltpu.with_memory_space_constraint(x, pltpu.HBM) for x in arguments])
        return advanced, landed.reshape(4, 1, 1, slots, capacity)

    placed = (
        P(None, "down", "cross", None),
        P(None, "down", "cross", None, None),
        P("down", "cross", None),
    )
    return jax.shard_map(
        local,
        mesh=mesh,
        in_specs=placed,
        out_specs=(P(None, "down", "cross", None), P(None, "down", "cross", None, None)),
        check_vma=False,
    )
```
